256 devices in a mesh: src: 8 (over y, core), tgt: 32 (over x, z).
Axes of the slice: x: 4, y: 4, z: 8, core: 2. Of those that a mesh axis runs over, the one named last changes fastest.
Arguments:
- coupling: bfloat16 [8192, 32768], P('src', 'tgt'), may hold values from 0.099609375 to 1
- cost_src: bfloat16 [8192, 1536], P('src'), may hold values from -0.15625 to 0.15625
- cost_tgt: bfloat16 [32768, 1536], P('tgt'), may hold values from -0.15625 to 0.15625
- pattern: int32 [32, 128], P('src', 'tgt'), may hold values from 0 to 1, as said below
- mass_src: float32 [8192], P('src'), may hold values from 0.5 to 2
- mass_tgt: float32 [32768], P('tgt'), may hold values from 0.5 to 2
Outputs:
- new_coupling: float32 [8192, 32768], P('src', 'tgt')
The draws below stay inside these ranges and needn't reach their ends.
Inputs may be any that keep to these rules, and one draw needn't show every extreme that they name: `pattern`: every row of tiles and every column of tiles holds at least one live tile.
All inputs are finite; a program needn't handle non-finite values.
Results may differ from the reference program's by a relative error of at most 0.0003.
Values may be sent and summed in bfloat16 or wider, within the bound.
No kernel may reach another device: no remote copies, remote signals or barrier semaphores. Data moves between devices by JAX's collectives and lax.ppermute only.
A program may use at most 64 MiB of HBM per device.

```python
import math
import jax
import jax.numpy as jnp
from jax import lax

TILE = 256
R_DEV = 1024
C_DEV = 1024
H1 = 256
H2 = 256
SRC_CELLS = 8192
TGT_CELLS = 32768
N_SRC = 8
N_TGT = 32


def draw_pattern(key, part):
    key = jax.random.fold_in(key, 11)
    tile_rows = SRC_CELLS // TILE
    tile_cols = TGT_CELLS // TILE
    key_level, key_roll = jax.random.split(key)
    level = jax.random.randint(key_level, (tile_rows, 1), 15, 85)
    rolled = jax.random.randint(key_roll, (tile_rows, tile_cols), 0, 100)
    row_index = jnp.arange(tile_rows, dtype=jnp.int32)[:, None]
    col_index = jnp.arange(tile_cols, dtype=jnp.int32)[None, :]
    alive = (rolled < level) | (col_index % tile_rows == row_index)
    return jnp.where(alive, 1, 0).astype(jnp.int32)


def level_of(stream_key, dims, cuts, least, high):
    gain = 1.0
    for axis_at, shards_of in cuts:
        draws = jax.random.uniform(jax.random.fold_in(jax.random.fold_in(stream_key, 6), axis_at), (shards_of,), jnp.float32, least / len(cuts), high / len(cuts))
        gain = gain * jnp.repeat(jnp.exp(draws), dims[axis_at] // shards_of).reshape((-1,) + (1,) * (len(dims) - 1 - axis_at))
    return gain


def noise(key, extent, deviation, reach, pieces=(), kind=jnp.bfloat16):
    drawn = jax.random.normal(key, extent, jnp.float32) * deviation
    if len(pieces) > 0:
        drawn = level_of(key, extent, pieces, -0.22, 0.18) * drawn
    return jnp.clip(drawn, min=-reach, max=reach).astype(kind)


def setup_inputs(seed: int = 0) -> dict:
    splits = jax.random.split(jax.random.key(seed), 7)
    coupling = jnp.clip(jnp.exp(math.log(1.0) - 2.306499 * jax.random.uniform(splits[0], (SRC_CELLS, TGT_CELLS), jnp.float32) ** level_of(splits[0], (SRC_CELLS, TGT_CELLS), ((0, 8), (1, 32)), -0.2, 0.2)), 0.099609375, 1.0).astype(jnp.bfloat16)
    cost_src = noise(splits[1], (SRC_CELLS, R_DEV + 2 * H1), (R_DEV + 2 * H1) ** -0.5, 0.15625, ((0, 8),))
    cost_tgt = noise(splits[2], (TGT_CELLS, C_DEV + 2 * H2), (C_DEV + 2 * H2) ** -0.5, 0.15625, ((0, 32),))
    pattern = draw_pattern(jax.random.fold_in(splits[6], 71), 0)
    mass_src = jnp.clip(jnp.exp(math.log(2.0) - 1.3862944 * jax.random.uniform(splits[4], (SRC_CELLS,), jnp.float32) ** level_of(splits[4], (SRC_CELLS,), ((0, 8),), -0.2, 0.2)), 0.5, 2.0)
    mass_tgt = jnp.clip(jnp.exp(math.log(2.0) - 1.3862944 * jax.random.uniform(splits[5], (TGT_CELLS,), jnp.float32) ** level_of(splits[5], (TGT_CELLS,), ((0, 32),), -0.2, 0.2)), 0.5, 2.0)
    return {"coupling": coupling, "cost_src": cost_src, "cost_tgt": cost_tgt, "pattern": pattern, "mass_src": mass_src, "mass_tgt": mass_tgt}


step_size = 1.0


def reference(coupling, cost_src, cost_tgt, pattern, mass_src, mass_tgt):
    tile_rows = SRC_CELLS // TILE
    tile_cols = TGT_CELLS // TILE
    gate_tiles = pattern.astype(jnp.bfloat16)[:, None, :, None]
    masked = (coupling.reshape(tile_rows, TILE, tile_cols, TILE) * gate_tiles).reshape(SRC_CELLS, TGT_CELLS)
    padded = jnp.pad(masked, ((H1, H1), (0, 0)))

    def row_block(block_index):
        start = (block_index * R_DEV).astype(jnp.int32)
        row_slab = lax.dynamic_slice_in_dim(padded, start, R_DEV + 2 * H1, 0)
        src_panel = lax.dynamic_slice_in_dim(cost_src, start, R_DEV, 0)
        return jnp.dot(src_panel, row_slab, preferred_element_type=jnp.float32)

    left_product = lax.map(row_block, jnp.arange(N_SRC, dtype=jnp.int32)).reshape(SRC_CELLS, TGT_CELLS)
    left_padded = jnp.pad(left_product, ((0, 0), (H2, H2)))

    def col_block(block_index):
        start = (block_index * C_DEV).astype(jnp.int32)
        col_slab = lax.dynamic_slice_in_dim(left_padded, start, C_DEV + 2 * H2, 1)
        tgt_panel = lax.dynamic_slice_in_dim(cost_tgt, start, C_DEV, 0).astype(jnp.float32)
        return lax.dot_general(col_slab, tgt_panel, (((1,), (1,)), ((), ())),
                               precision=lax.Precision.HIGHEST, preferred_element_type=jnp.float32)

    grad_blocks = lax.map(col_block, jnp.arange(N_TGT, dtype=jnp.int32))
    grad_field = jnp.moveaxis(grad_blocks, 0, 1).reshape(SRC_CELLS, TGT_CELLS)
    kernel = masked.astype(jnp.float32) * jnp.exp(step_size * grad_field)
    row_total = jnp.sum(kernel, axis=1)
    scaled = kernel * (mass_src * TGT_CELLS / row_total)[:, None]
    col_total = jnp.sum(scaled, axis=0)
    return scaled * (mass_tgt * SRC_CELLS / col_total)[None, :]
```

```python
import jax
import jax.numpy as jnp
from jax import lax
from jax.sharding import PartitionSpec as P

TILE = 256
H1 = 256
H2 = 256


step_size = 1.0


def pair_plans(size):
    near = [(i, i ^ 1) for i in range(size)]
    far = []
    for i in range(1, size - 1, 2):
        far += [(i, i + 1), (i + 1, i)]
    return near, far


def exchange(first, second, axis):
    near, far = pair_plans(lax.axis_size(axis))
    return lax.ppermute(first, axis, near), lax.ppermute(second, axis, far)


def total_over(x, axis):
    size = lax.axis_size(axis)
    copies = jnp.broadcast_to(x[None, :], (size, x.shape[0]))
    copies = lax.optimization_barrier(copies)
    return jnp.sum(lax.all_to_all(copies, axis, 0, 0), axis=0)


def split_dot(a, b):
    hi = lax.reduce_precision(a, 8, 7)
    lo = (a - hi).astype(jnp.bfloat16)
    dims = (((1,), (1,)), ((), ()))
    dot = lambda x: lax.dot_general(x, b, dims, preferred_element_type=jnp.float32)
    return dot(hi.astype(jnp.bfloat16)) + dot(lo)


def per_device(coupling, cost_src, cost_tgt, pattern, mass_src, mass_tgt):
    rows, cols = coupling.shape
    n_src, n_tgt = lax.axis_size("src"), lax.axis_size("tgt")
    odd_s = lax.axis_index("src") % 2
    odd_t = lax.axis_index("tgt") % 2

    row_tile = lax.broadcasted_iota(jnp.int32, (rows, cols), 0) // TILE
    col_tile = lax.broadcasted_iota(jnp.int32, (rows, cols), 1) // TILE
    gate = jnp.zeros((rows, cols), jnp.int32)
    for r in range(pattern.shape[0]):
        for c in range(pattern.shape[1]):
            gate = jnp.where((row_tile == r) & (col_tile == c), pattern[r, c], gate)
    masked = jnp.where(gate != 0, coupling, jnp.zeros_like(coupling))

    c_near = (1 - odd_t) * (cols - H2)
    c_far = odd_t * (cols - H2)
    r_near = (1 - odd_s) * (rows - H1)
    r_far = odd_s * (rows - H1)
    side = exchange(
        lax.dynamic_slice_in_dim(masked, c_near, H2, 1),
        lax.dynamic_slice_in_dim(masked, c_far, H2, 1),
        "tgt",
    )
    ends = exchange(
        lax.dynamic_slice_in_dim(masked, r_near, H1, 0),
        lax.dynamic_slice_in_dim(masked, r_far, H1, 0),
        "src",
    )
    sides = jnp.concatenate(side, axis=1)
    corners = exchange(
        lax.dynamic_slice_in_dim(sides, r_near, H1, 0),
        lax.dynamic_slice_in_dim(sides, r_far, H1, 0),
        "src",
    )

    s_own = cost_src[:, H1:H1 + rows]
    s_near = lax.dynamic_slice_in_dim(cost_src, (1 - odd_s) * (rows + H1), H1, 1)
    s_far = lax.dynamic_slice_in_dim(cost_src, odd_s * (rows + H1), H1, 1)
    t_own = cost_tgt[:, H2:H2 + cols]
    t_near = lax.dynamic_slice_in_dim(cost_tgt, (1 - odd_t) * (cols + H2), H2, 1)
    t_far = lax.dynamic_slice_in_dim(cost_tgt, odd_t * (cols + H2), H2, 1)
    s_ends = jnp.concatenate([s_near, s_far], axis=1)
    t_sides = jnp.concatenate([t_near, t_far], axis=1)

    dot = lambda a, b: jnp.dot(a, b, preferred_element_type=jnp.float32)
    left_own = dot(s_own, masked) + dot(s_ends, jnp.concatenate(ends, axis=0))
    grad = split_dot(left_own, t_own)
    left_sides = dot(s_own, sides) + dot(s_ends, jnp.concatenate(corners, axis=0))
    grad = grad + split_dot(left_sides, t_sides)

    kernel = masked.astype(jnp.float32) * jnp.exp(step_size * grad)
    row_total = total_over(jnp.sum(kernel, axis=1), "tgt")
    scaled = kernel * (mass_src * (cols * n_tgt) / row_total)[:, None]
    col_total = total_over(jnp.sum(scaled, axis=0), "src")
    return scaled * (mass_tgt * (rows * n_src) / col_total)[None, :]


def solution(mesh):
    return jax.shard_map(
        per_device,
        mesh=mesh,
        in_specs=(
            P("src", "tgt"),
            P("src", None),
            P("tgt", None),
            P("src", "tgt"),
            P("src"),
            P("tgt"),
        ),
        out_specs=P("src", "tgt"),
        check_vma=False,
    )
```

```python
import jax
import jax.numpy as jnp
from jax import lax
from jax.experimental import pallas as pl
from jax.experimental.pallas import tpu as pltpu
from jax.sharding import PartitionSpec as P

TILE = 256
H1 = 256
H2 = 256
LANES = 128

step_size = 1.0

f32 = jnp.float32
bf16 = jnp.bfloat16
VMEM = pltpu.VMEM
MIB = 1 << 20


def odd(axis):
    return lax.rem(lax.axis_index(axis), 2)


def at(parity, last):
    return pl.multiple_of(parity * last, TILE)


def dot(a, b):
    return jnp.dot(a, b, preferred_element_type=f32)


def dot_t(a, b):
    return lax.dot_general(a, b, (((1,), (1,)), ((), ())), preferred_element_type=f32)


def halves(x):
    hi = x.astype(bf16)
    return hi, (x - hi.astype(f32)).astype(bf16)


def as_row(x):
    return jnp.sum(x.T, axis=0, keepdims=True)


def mask_kernel(pattern, coupling, masked, c_near, c_far, r_near, r_far, raw, sems):
    rows, cols = masked.shape
    tiles_r, tiles_c = rows // TILE, cols // TILE

    def copy(r):
        part = pl.ds(r * TILE, TILE)
        return pltpu.make_async_copy(coupling.at[part], raw.at[part], sems.at[r])

    for r in range(tiles_r):
        copy(r).start()
    odd_s, odd_t = odd("src"), odd("tgt")
    c_last, r_last = cols - H2, rows - H1
    for r in range(tiles_r):
        copy(r).wait()
        part = slice(r * TILE, (r + 1) * TILE)
        for c in range(tiles_c):
            across = slice(c * TILE, (c + 1) * TILE)
            tile = raw[part, across]
            masked[part, across] = jnp.where(pattern[r, c] != 0, tile, jnp.zeros_like(tile))
        c_near[part, :] = masked[part, pl.ds(at(1 - odd_t, c_last), H2)]
        c_far[part, :] = masked[part, pl.ds(at(odd_t, c_last), H2)]
    r_near[...] = masked[pl.ds(at(1 - odd_s, r_last), H1), :]
    r_far[...] = masked[pl.ds(at(odd_s, r_last), H1), :]


def left_kernel(masked, r_near, r_far, cost_src, hi, lo):
    rows, cols = masked.shape
    odd_s = odd("src")
    s_near = pl.ds(at(1 - odd_s, rows + H1), H1)
    s_far = pl.ds(at(odd_s, rows + H1), H1)

    @pl.loop(0, cols // TILE)
    def _(n):
        across = pl.ds(pl.multiple_of(n * TILE, TILE), TILE)
        left = dot(cost_src[:, H1:H1 + rows], masked[:, across])
        left += dot(cost_src[:, s_near], r_near[:, across])
        left += dot(cost_src[:, s_far], r_far[:, across])
        hi[:, across], lo[:, across] = halves(left)


def own_kernel(hi, lo, cost_tgt, grad):
    rows, cols = grad.shape

    @pl.loop(0, cols // TILE)
    def _(n):
        across = pl.ds(pl.multiple_of(n * TILE, TILE), TILE)
        costs = cost_tgt[across, H2:H2 + cols]
        grad[:, across] = dot_t(hi[...], costs) + dot_t(lo[...], costs)


def tail_kernel(c_near, c_far, x_near, x_far, cost_src, cost_tgt, grad, masked,
                kernel, totals, hi, lo, part):
    rows, cols = masked.shape
    odd_s, odd_t = odd("src"), odd("tgt")
    s_near = pl.ds(at(1 - odd_s, rows + H1), H1)
    s_far = pl.ds(at(odd_s, rows + H1), H1)
    for n, side in ((0, c_near), (1, c_far)):
        across = slice(n * H2, (n + 1) * H2)
        left = dot(cost_src[:, H1:H1 + rows], side[...])
        left += dot(cost_src[:, s_near], x_near[:, across])
        left += dot(cost_src[:, s_far], x_far[:, across])
        hi[:, across], lo[:, across] = halves(left)
    part[...] = jnp.zeros_like(part)

    @pl.loop(0, cols // TILE)
    def _(n):
        across = pl.ds(pl.multiple_of(n * TILE, TILE), TILE)
        g = grad[:, across]
        for k, start in ((0, 1 - odd_t), (1, odd_t)):
            of = slice(k * H2, (k + 1) * H2)
            costs = cost_tgt[across, pl.ds(at(start, cols + H2), H2)]
            g += dot_t(hi[:, of], costs) + dot_t(lo[:, of], costs)
        value = masked[:, across].astype(f32) * jnp.exp(step_size * g)
        kernel[:, across] = value
        part[...] += value[:, :LANES] + value[:, LANES:]

    totals[...] = jnp.broadcast_to(as_row(part[...]), totals.shape)


def column_kernel(total, row_totals, mass, kernel, scaled, totals):
    rows, cols = kernel.shape
    factor = mass[...] * total / jnp.sum(row_totals[...], axis=0, keepdims=True)
    factor = jnp.broadcast_to(factor, (LANES, rows)).T
    for n in range(cols // LANES):
        across = slice(n * LANES, (n + 1) * LANES)
        value = kernel[:, across] * factor
        scaled[:, across] = value
        sums = jnp.sum(value, axis=0, keepdims=True)
        totals[:, across] = jnp.broadcast_to(sums, (totals.shape[0], LANES))


def last_kernel(total, col_totals, mass, scaled, out, block, sems):
    rows, cols = scaled.shape
    factor = mass[...] * total / jnp.sum(col_totals[...], axis=0, keepdims=True)
    n_blocks = sems.shape[0]
    size = rows // n_blocks

    def copy(n):
        part = pl.ds(n * size, size)
        return pltpu.make_async_copy(block.at[part], out.at[part], sems.at[n])

    for n in range(n_blocks):
        part = slice(n * size, (n + 1) * size)
        block[part, :] = scaled[part, :] * factor
        copy(n).start()
    for n in range(n_blocks):
        copy(n).wait()


def call(body, inputs, outputs, scratch, spaces=None, limit=16, flops=0, moved=0, exps=0):
    spaces = spaces or [VMEM] * len(inputs)
    args = [
        pltpu.with_memory_space_constraint(x, VMEM) if s is VMEM else x
        for x, s in zip(inputs, spaces)
    ]
    single = len(outputs) == 1
    shapes = [s if isinstance(s, jax.ShapeDtypeStruct) else VMEM(*s) for s in outputs]
    out_specs = [
        pl.BlockSpec(memory_space=pl.ANY if isinstance(s, jax.ShapeDtypeStruct) else VMEM)
        for s in outputs
    ]
    return pl.pallas_call(
        body,
        out_shape=shapes[0] if single else shapes,
        in_specs=[pl.BlockSpec(memory_space=s) for s in spaces],
        out_specs=out_specs[0] if single else out_specs,
        scratch_shapes=scratch,
        cost_estimate=pl.CostEstimate(flops=flops, bytes_accessed=moved, transcendentals=exps),
        compiler_params=pltpu.CompilerParams(vmem_limit_bytes=limit * MIB),
    )(*args)


def pair_plans(size):
    near = [(i, i ^ 1) for i in range(size)]
    far = []
    for i in range(1, size - 1, 2):
        far += [(i, i + 1), (i + 1, i)]
    return near, far


def exchange(first, second, axis):
    near, far = pair_plans(lax.axis_size(axis))
    return lax.ppermute(first, axis, near), lax.ppermute(second, axis, far)


def per_device(coupling, cost_src, cost_tgt, pattern, mass_src, mass_tgt):
    rows, cols = coupling.shape
    n_src, n_tgt = lax.axis_size("src"), lax.axis_size("tgt")
    tiles = pattern.shape[0]
    dma = pltpu.SemaphoreType.DMA

    masked, c_near, c_far, r_near, r_far = call(
        mask_kernel,
        [pattern, coupling],
        [((rows, cols), bf16)] + [((rows, H2), bf16)] * 2 + [((H1, cols), bf16)] * 2,
        [VMEM((rows, cols), bf16), dma((tiles,))],
        spaces=[pltpu.SMEM, pl.ANY],
        moved=6 * MIB,
    )
    c_near, c_far = exchange(c_near, c_far, "tgt")
    r_near, r_far = exchange(r_near, r_far, "src")
    hi, lo = call(
        left_kernel,
        [masked, r_near, r_far, cost_src],
        [((rows, cols), bf16)] * 2,
        [],
        flops=2 * rows * cols * (cols + 2 * H1),
        moved=10 * MIB,
    )
    c_near, c_far, hi, lo = lax.optimization_barrier((c_near, c_far, hi, lo))

    def corners(start):
        pick = lambda x: lax.dynamic_slice_in_dim(x, start, H1, 0)
        return jnp.concatenate([pick(c_near), pick(c_far)], axis=1)

    odd_s = odd("src")
    x_near, x_far = exchange(
        corners((1 - odd_s) * (rows - H1)), corners(odd_s * (rows - H1)), "src"
    )
    grad = call(
        own_kernel,
        [hi, lo, cost_tgt],
        [((rows, cols), f32)],
        [],
        flops=4 * rows * cols * cols,
        moved=10 * MIB,
    )
    kernel, totals = call(
        tail_kernel,
        [c_near, c_far, x_near, x_far, cost_src, cost_tgt, grad, masked],
        [((rows, cols), f32), ((n_tgt, rows), f32)],
        [VMEM((rows, 2 * H2), bf16)] * 2 + [VMEM((rows, LANES), f32)],
        flops=2 * rows * 2 * H2 * (3 * cols + 2 * H1),
        moved=16 * MIB,
        exps=rows * cols,
    )
    row_totals = lax.all_to_all(totals, "tgt", 0, 0, tiled=True)
    scaled, totals = call(
        lambda *refs: column_kernel(float(cols * n_tgt), *refs),
        [row_totals, mass_src[None, :], kernel],
        [((rows, cols), f32), ((n_src, cols), f32)],
        [],
        moved=8 * MIB,
    )
    col_totals = lax.all_to_all(totals, "src", 0, 0, tiled=True)
    return call(
        lambda *refs: last_kernel(float(rows * n_src), *refs),
        [col_totals, mass_tgt[None, :], scaled],
        [jax.ShapeDtypeStruct((rows, cols), f32)],
        [VMEM((rows, cols), f32), dma((8,))],
        moved=8 * MIB,
    )


def solution(mesh):
    return jax.shard_map(
        per_device,
        mesh=mesh,
        in_specs=(
            P("src", "tgt"),
            P("src", None),
            P("tgt", None),
            P("src", "tgt"),
            P("src"),
            P("tgt"),
        ),
        out_specs=P("src", "tgt"),
        check_vma=False,
    )
```

```python
import jax
import jax.numpy as jnp
from jax import lax
from jax.experimental import pallas as pl
from jax.experimental.pallas import tpu as pltpu
from jax.sharding import PartitionSpec as P

TILE = 256
H1 = 256
H2 = 256
LANES = 128

step_size = 1.0

f32 = jnp.float32
bf16 = jnp.bfloat16
VMEM = pltpu.VMEM
MIB = 1 << 20


def odd(axis):
    return lax.rem(lax.axis_index(axis), 2) == 1


def dot(a, b):
    return jnp.dot(a, b, preferred_element_type=f32)


def dot_t(a, b):
    return lax.dot_general(a, b, (((1,), (1,)), ((), ())), preferred_element_type=f32)


def halves(x):
    hi = x.astype(bf16)
    return hi, (x - hi.astype(f32)).astype(bf16)


def as_row(x):
    return jnp.sum(x.T, axis=0, keepdims=True)


def tiles_of(size):
    return [slice(n * TILE, (n + 1) * TILE) for n in range(size // TILE)]


def side_kernel(pattern, coupling, masked, c_near, c_far, raw, gates, sems, sem):
    rows, cols = masked.shape
    down, along = tiles_of(rows), tiles_of(cols)
    gate = pltpu.make_async_copy(pattern, gates, sem)
    copies = [
        pltpu.make_async_copy(coupling.at[part], raw.at[part], sems.at[r])
        for r, part in enumerate(down)
    ]
    for copy in copies:
        copy.start()
    gate.start()
    odd_t = odd("tgt")
    gate.wait()
    for r, part in enumerate(down):
        copies[r].wait()
        for c, across in enumerate(along):
            tile = raw[part, across]
            masked[part, across] = jnp.where(gates[r, c] != 0, tile, jnp.zeros_like(tile))
        first, last = masked[part, along[0]], masked[part, along[-1]]
        c_near[part, :] = jnp.where(odd_t, first, last)
        c_far[part, :] = jnp.where(odd_t, last, first)


def band_copies(band, own, width, parity, out, sems):
    last = own + width
    near = pl.multiple_of((1 - parity) * last, TILE)
    far = pl.multiple_of(parity * last, TILE)
    spans = [(width, own, 0), (near, width, own), (far, width, own + width)]
    return [
        pltpu.make_async_copy(
            band.at[:, pl.ds(start, size)], out.at[:, pl.ds(to, size)], sems.at[n]
        )
        for n, (start, size, to) in enumerate(spans)
    ]


def end_kernel(masked, src_hbm, r_near, r_far, cost_src, sems):
    rows, cols = masked.shape
    copies = band_copies(src_hbm, rows, H1, odd("src").astype(jnp.int32), cost_src, sems)
    for copy in copies:
        copy.start()
    first, last = masked[:H1, :], masked[rows - H1:, :]
    odd_s = odd("src")
    r_near[...] = jnp.where(odd_s, first, last)
    r_far[...] = jnp.where(odd_s, last, first)
    for copy in copies:
        copy.wait()


def local_kernel(masked, cost_src, tgt_hbm, grad, cost_tgt, hi, lo, sems):
    rows, cols = masked.shape
    copies = band_copies(tgt_hbm, cols, H2, odd("tgt").astype(jnp.int32), cost_tgt, sems)
    for copy in copies:
        copy.start()
    for across in tiles_of(cols):
        hi[:, across], lo[:, across] = halves(dot(cost_src[:, :rows], masked[:, across]))
    for copy in copies:
        copy.wait()
    for across in tiles_of(cols):
        costs = cost_tgt[across, :cols]
        both = jnp.concatenate([hi[...], lo[...]], axis=1)
        grad[:, across] = dot_t(both, jnp.concatenate([costs, costs], axis=1))


def corner_kernel(c_near, c_far, x_near, x_far):
    rows = c_near.shape[0]
    odd_s = odd("src")
    for n, side in enumerate((c_near, c_far)):
        across = slice(n * H2, (n + 1) * H2)
        first, last = side[:H1, :], side[rows - H1:, :]
        x_near[:, across] = jnp.where(odd_s, first, last)
        x_far[:, across] = jnp.where(odd_s, last, first)


def halo_kernel(c_near, c_far, r_near, r_far, cost_src, cost_tgt, grad,
                out, ends, hi, lo):
    rows, cols = grad.shape
    for n, side in enumerate((c_near, c_far)):
        across = slice(n * H2, (n + 1) * H2)
        hi[:, across], lo[:, across] = halves(dot(cost_src[:, :rows], side[...]))
    for across in tiles_of(cols):
        costs = cost_tgt[across, cols:]
        both = jnp.concatenate([hi[...], lo[...]], axis=1)
        out[:, across] = grad[:, across] + dot_t(both, jnp.concatenate([costs, costs], axis=1))
    rim = jnp.concatenate([r_near[...], r_far[...]], axis=0)
    for across in tiles_of(cols):
        ends[:, across] = dot_t(rim, cost_tgt[across, :cols])


def tail_kernel(x_near, x_far, cost_src, cost_tgt, ends, grad, masked, kernel, totals, part):
    rows, cols = masked.shape
    corners = jnp.concatenate([x_near[...], x_far[...]], axis=0)
    bands = cost_src[:, rows:]
    bands = jnp.concatenate([bands, bands], axis=1)
    for n, across in enumerate(tiles_of(cols)):
        hi, lo = halves(ends[:, across] + dot_t(corners, cost_tgt[across, cols:]))
        slope = grad[:, across] + dot(bands, jnp.concatenate([hi, lo], axis=0))
        value = masked[:, across].astype(f32) * jnp.exp(step_size * slope)
        kernel[:, across] = value
        sums = value[:, :LANES] + value[:, LANES:]
        part[...] = sums if n == 0 else part[...] + sums
    totals[...] = jnp.broadcast_to(as_row(part[...]), totals.shape)


def column_kernel(total, row_totals, mass, kernel, scaled, totals):
    rows, cols = kernel.shape
    factor = mass[...] * total / jnp.sum(row_totals[...], axis=0, keepdims=True)
    factor = jnp.broadcast_to(factor, (LANES, rows)).T
    for n in range(cols // LANES):
        across = slice(n * LANES, (n + 1) * LANES)
        value = kernel[:, across] * factor
        scaled[:, across] = value
        sums = jnp.sum(value, axis=0, keepdims=True)
        totals[:, across] = jnp.broadcast_to(sums, (totals.shape[0], LANES))


def last_kernel(total, col_totals, mass, scaled, out, block, sems):
    rows, cols = scaled.shape
    factor = mass[...] * total / jnp.sum(col_totals[...], axis=0, keepdims=True)
    n_blocks = sems.shape[0]
    size = rows // n_blocks

    def copy(n):
        part = pl.ds(n * size, size)
        return pltpu.make_async_copy(block.at[part], out.at[part], sems.at[n])

    for n in range(n_blocks):
        part = slice(n * size, (n + 1) * size)
        block[part, :] = scaled[part, :] * factor
        copy(n).start()
    for n in range(n_blocks):
        copy(n).wait()


def call(body, inputs, outputs, scratch, far=(), limit=12, flops=0, moved=0, exps=0):
    args, in_specs = [], []
    for n, x in enumerate(inputs):
        args.append(pltpu.with_memory_space_constraint(x, pltpu.HBM if n in far else VMEM))
        in_specs.append(pl.BlockSpec(memory_space=pl.ANY if n in far else VMEM))
    is_far = [isinstance(s, jax.ShapeDtypeStruct) for s in outputs]
    shapes = [s if f else VMEM(*s) for s, f in zip(outputs, is_far)]
    out_specs = [pl.BlockSpec(memory_space=pl.ANY if f else VMEM) for f in is_far]
    single = len(outputs) == 1
    return pl.pallas_call(
        body,
        out_shape=shapes[0] if single else shapes,
        in_specs=in_specs,
        out_specs=out_specs[0] if single else out_specs,
        scratch_shapes=scratch,
        cost_estimate=pl.CostEstimate(flops=flops, bytes_accessed=moved, transcendentals=exps),
        compiler_params=pltpu.CompilerParams(vmem_limit_bytes=limit * MIB),
    )(*args)


def pair_plans(size):
    near = [(i, i ^ 1) for i in range(size)]
    far = []
    for i in range(1, size - 1, 2):
        far += [(i, i + 1), (i + 1, i)]
    return near, far


def exchange(first, second, axis):
    near, far = pair_plans(lax.axis_size(axis))
    return lax.ppermute(first, axis, near), lax.ppermute(second, axis, far)


def per_device(coupling, cost_src, cost_tgt, pattern, mass_src, mass_tgt):
    rows, cols = coupling.shape
    n_src, n_tgt = lax.axis_size("src"), lax.axis_size("tgt")
    tiles = pattern.shape[0]
    dma = pltpu.SemaphoreType.DMA

    masked, c_near, c_far = call(
        side_kernel,
        [pattern, coupling],
        [((rows, cols), bf16)] + [((rows, H2), bf16)] * 2,
        [
            VMEM((rows, cols), bf16),
            pltpu.SMEM(pattern.shape, pattern.dtype),
            dma((tiles,)),
            dma,
        ],
        far=(0, 1),
        moved=6 * MIB,
    )
    c_near, c_far = exchange(c_near, c_far, "tgt")
    r_near, r_far, cost_src = call(
        end_kernel,
        [masked, cost_src],
        [((H1, cols), bf16)] * 2 + [(cost_src.shape, bf16)],
        [dma((3,))],
        far=(1,),
        moved=5 * MIB,
    )
    r_near, r_far = exchange(r_near, r_far, "src")
    grad, cost_tgt = call(
        local_kernel,
        [masked, cost_src, cost_tgt],
        [((rows, cols), f32), (cost_tgt.shape, bf16)],
        [VMEM((rows, cols), bf16)] * 2 + [dma((3,))],
        far=(2,),
        moved=MIB,
    )

    x_near, x_far = call(
        corner_kernel,
        [c_near, c_far],
        [((H1, 2 * H2), bf16)] * 2,
        [],
        moved=1024 * MIB,
    )
    x_near, x_far = exchange(x_near, x_far, "src")
    grad, ends = call(
        halo_kernel,
        [c_near, c_far, r_near, r_far, cost_src, cost_tgt, grad],
        [((rows, cols), f32), ((2 * H1, cols), f32)],
        [VMEM((rows, 2 * H2), bf16)] * 2,
        flops=2 * rows * cols * (2 * H1 + 6 * H2),
        moved=10 * MIB,
    )
    kernel, totals = call(
        tail_kernel,
        [x_near, x_far, cost_src, cost_tgt, ends, grad, masked],
        [((rows, cols), f32), ((n_tgt, rows), f32)],
        [VMEM((rows, LANES), f32)],
        flops=2 * rows * cols * (4 * H1 + H2),
        moved=16 * MIB,
        exps=rows * cols,
    )
    row_totals = lax.all_to_all(totals, "tgt", 0, 0, tiled=True)
    scaled, totals = call(
        lambda *refs: column_kernel(float(cols * n_tgt), *refs),
        [row_totals, mass_src[None, :], kernel],
        [((rows, cols), f32), ((n_src, cols), f32)],
        [],
        moved=8 * MIB,
    )
    col_totals = lax.all_to_all(totals, "src", 0, 0, tiled=True)
    return call(
        lambda *refs: last_kernel(float(rows * n_src), *refs),
        [col_totals, mass_tgt[None, :], scaled],
        [jax.ShapeDtypeStruct((rows, cols), f32)],
        [VMEM((rows, cols), f32), dma((8,))],
        moved=8 * MIB,
    )


def solution(mesh):
    return jax.shard_map(
        per_device,
        mesh=mesh,
        in_specs=(
            P("src", "tgt"),
            P("src", None),
            P("tgt", None),
            P("src", "tgt"),
            P("src"),
            P("tgt"),
        ),
        out_specs=P("src", "tgt"),
        check_vma=False,
    )
```

```python
import jax
import jax.numpy as jnp
from jax import lax
from jax.experimental import pallas as pl
from jax.experimental.pallas import tpu as pltpu
from jax.sharding import PartitionSpec as P

TILE = 256
H1 = 256
H2 = 256
LANES = 128

step_size = 1.0

f32 = jnp.float32
bf16 = jnp.bfloat16
VMEM = pltpu.VMEM
MIB = 1 << 20
EST = dict(side=6 * MIB, end=2 * MIB, left=MIB, corner=MIB, ends=MIB, own=MIB, sides=MIB, tail=MIB)


def odd(axis):
    return lax.rem(lax.axis_index(axis), 2) == 1


def at_end(axis):
    index = lax.axis_index(axis)
    return (index == 0) | (index == lax.axis_size(axis) - 1)


def dot(a, b):
    return jnp.dot(a, b, preferred_element_type=f32)


def dot_t(a, b):
    return lax.dot_general(a, b, (((1,), (1,)), ((), ())), preferred_element_type=f32)


def halves(x):
    hi = x.astype(bf16)
    return hi, (x - hi.astype(f32)).astype(bf16)


def as_row(x):
    return jnp.sum(x.T, axis=0, keepdims=True)


def tiles_of(size):
    return [slice(n * TILE, (n + 1) * TILE) for n in range(size // TILE)]


def side_kernel(pattern, coupling, masked, e_near, e_far, raw, gates, sems, sem):
    rows, cols = masked.shape
    down, along = tiles_of(rows), tiles_of(cols)
    gate = pltpu.make_async_copy(pattern, gates, sem)
    copies = [
        pltpu.make_async_copy(coupling.at[part], raw.at[part], sems.at[r])
        for r, part in enumerate(down)
    ]
    for copy in copies:
        copy.start()
    gate.start()
    odd_t = odd("tgt")
    gate.wait()
    for r, part in enumerate(down):
        copies[r].wait()
        for c, across in enumerate(along):
            tile = raw[part, across]
            masked[part, across] = jnp.where(gates[r, c] != 0, tile, jnp.zeros_like(tile))
        if r in (0, len(down) - 1):
            to = slice(0, H1) if r == 0 else slice(H1, 2 * H1)
            first, last = masked[part, along[0]], masked[part, along[-1]]
            e_near[to, :] = jnp.where(odd_t, first, last)
            e_far[to, :] = jnp.where(odd_t, last, first)


def end_kernel(masked, r_near, r_far):
    rows, cols = masked.shape
    first, last = masked[:H1, :], masked[rows - H1:, :]
    odd_s = odd("src")
    r_near[...] = jnp.where(odd_s, first, last)
    r_far[...] = jnp.where(odd_s, last, first)


def by_nearness(band, own, width, parity, out):
    first, last = band[:, :width], band[:, own + width:]
    out[:, :width] = jnp.where(parity, first, last)
    out[:, width:] = jnp.where(parity, last, first)


def band_copies(band, own, width, parity, out, sems):
    last = own + width
    near = pl.multiple_of((1 - parity) * last, TILE)
    far = pl.multiple_of(parity * last, TILE)
    spans = [(width, own, 0), (near, width, own), (far, width, own + width)]
    return [
        pltpu.make_async_copy(
            band.at[:, pl.ds(start, size)], out.at[:, pl.ds(to, size)], sems.at[n]
        )
        for n, (start, size, to) in enumerate(spans)
    ]


def left_kernel(masked, r_near, cost_src, tgt_hbm, m_near, m_far, left, src_ends, cost_tgt, sems):
    rows, cols = masked.shape
    odd_t = odd("tgt")
    copies = band_copies(tgt_hbm, cols, H2, odd_t.astype(jnp.int32), cost_tgt, sems)
    for copy in copies:
        copy.start()
    first, last = masked[H1:rows - H1, :H2], masked[H1:rows - H1, cols - H2:]
    m_near[...] = jnp.where(odd_t, first, last)
    m_far[...] = jnp.where(odd_t, last, first)
    by_nearness(cost_src, rows, H1, odd("src"), src_ends)

    @pl.when(at_end("src"))
    def _():
        src_ends[:, H1:] = jnp.zeros((rows, H1), bf16)

    for across in tiles_of(cols):
        bands = jnp.concatenate([cost_src[:, H1:H1 + rows], src_ends[:, :H1]], axis=1)
        column = jnp.concatenate([masked[:, across], r_near[:, across]], axis=0)
        left[:, across] = dot(bands, column)
    for copy in copies:
        copy.wait()

    @pl.when(at_end("tgt"))
    def _():
        cost_tgt[:, cols + H2:] = jnp.zeros((cols, H2), bf16)


def corner_kernel(e_near, e_far, _, x_near, x_far):
    odd_s = odd("src")
    for n, side in enumerate((e_near, e_far)):
        across = slice(n * H2, (n + 1) * H2)
        first, last = side[:H1, :], side[H1:, :]
        x_near[:, across] = jnp.where(odd_s, first, last)
        x_far[:, across] = jnp.where(odd_s, last, first)


def ends_kernel(left, r_far, src_ends, hi, lo):
    rows, cols = left.shape
    for across in tiles_of(cols):
        value = left[:, across] + dot(src_ends[:, H1:], r_far[:, across])
        hi[:, across], lo[:, across] = halves(value)


def own_kernel(hi, lo, cost_tgt, grad):
    rows, cols = grad.shape
    both = jnp.concatenate([hi[...], lo[...]], axis=1)
    for across in tiles_of(cols):
        costs = cost_tgt[across, :cols]
        grad[:, across] = dot_t(both, jnp.concatenate([costs, costs], axis=1))


def sides_kernel(e_near, e_far, m_near, m_far, cost_src, sides):
    rows = cost_src.shape[0]
    for n, (e, m) in enumerate(((e_near, m_near), (e_far, m_far))):
        column = jnp.concatenate([e[:H1, :], m[...], e[H1:, :]], axis=0)
        sides[:, n * H2:(n + 1) * H2] = dot(cost_src[:, H1:H1 + rows], column)


def tail_kernel(x_near, x_far, sides, src_ends, cost_tgt, grad, masked,
                kernel, totals, hi, lo, part):
    rows, cols = masked.shape
    for across in tiles_of(2 * H2):
        corners = jnp.concatenate([x_near[:, across], x_far[:, across]], axis=0)
        hi[:, across], lo[:, across] = halves(sides[:, across] + dot(src_ends[...], corners))
    both = jnp.concatenate([hi[...], lo[...]], axis=1)
    for n, across in enumerate(tiles_of(cols)):
        costs = cost_tgt[across, cols:]
        slope = grad[:, across] + dot_t(both, jnp.concatenate([costs, costs], axis=1))
        value = masked[:, across].astype(f32) * jnp.exp(step_size * slope)
        kernel[:, across] = value
        sums = value[:, :LANES] + value[:, LANES:]
        part[...] = sums if n == 0 else part[...] + sums
    totals[...] = jnp.broadcast_to(as_row(part[...]), totals.shape)


def column_kernel(total, row_totals, mass, kernel, scaled, totals):
    rows, cols = kernel.shape
    factor = mass[...] * total / jnp.sum(row_totals[...], axis=0, keepdims=True)
    factor = jnp.broadcast_to(factor, (LANES, rows)).T
    for n in range(cols // LANES):
        across = slice(n * LANES, (n + 1) * LANES)
        value = kernel[:, across] * factor
        scaled[:, across] = value
        sums = jnp.sum(value, axis=0, keepdims=True)
        totals[:, across] = jnp.broadcast_to(sums, (totals.shape[0], LANES))


def last_kernel(total, col_totals, mass, scaled, out, block, sems):
    rows, cols = scaled.shape
    factor = mass[...] * total / jnp.sum(col_totals[...], axis=0, keepdims=True)
    n_blocks = sems.shape[0]
    size = rows // n_blocks

    def copy(n):
        part = pl.ds(n * size, size)
        return pltpu.make_async_copy(block.at[part], out.at[part], sems.at[n])

    for n in range(n_blocks):
        part = slice(n * size, (n + 1) * size)
        block[part, :] = scaled[part, :] * factor
        copy(n).start()
    for n in range(n_blocks):
        copy(n).wait()


def call(body, inputs, outputs, scratch, far=(), limit=12, flops=0, moved=0, exps=0):
    args, in_specs = [], []
    for n, x in enumerate(inputs):
        args.append(pltpu.with_memory_space_constraint(x, pltpu.HBM if n in far else VMEM))
        in_specs.append(pl.BlockSpec(memory_space=pl.ANY if n in far else VMEM))
    is_far = [isinstance(s, jax.ShapeDtypeStruct) for s in outputs]
    shapes = [s if f else VMEM(*s) for s, f in zip(outputs, is_far)]
    out_specs = [pl.BlockSpec(memory_space=pl.ANY if f else VMEM) for f in is_far]
    single = len(outputs) == 1
    return pl.pallas_call(
        body,
        out_shape=shapes[0] if single else shapes,
        in_specs=in_specs,
        out_specs=out_specs[0] if single else out_specs,
        scratch_shapes=scratch,
        cost_estimate=pl.CostEstimate(flops=flops, bytes_accessed=moved, transcendentals=exps),
        compiler_params=pltpu.CompilerParams(vmem_limit_bytes=limit * MIB),
    )(*args)


def pair_plans(size):
    near = [(i, i ^ 1) for i in range(size)]
    far = [(i, (i + 1 if i % 2 else i - 1) % size) for i in range(size)]
    return near, far


def exchange(first, second, axis):
    near, far = pair_plans(lax.axis_size(axis))
    return lax.ppermute(first, axis, near), lax.ppermute(second, axis, far)


def per_device(coupling, cost_src, cost_tgt, pattern, mass_src, mass_tgt):
    rows, cols = coupling.shape
    n_src, n_tgt = lax.axis_size("src"), lax.axis_size("tgt")
    tiles = pattern.shape[0]
    dma = pltpu.SemaphoreType.DMA

    masked, e_near, e_far = call(
        side_kernel,
        [pattern, coupling],
        [((rows, cols), bf16)] + [((2 * H1, H2), bf16)] * 2,
        [
            VMEM((rows, cols), bf16),
            pltpu.SMEM(pattern.shape, pattern.dtype),
            dma((tiles,)),
            dma,
        ],
        far=(0, 1),
        moved=EST["side"],
    )
    e_near, e_far = exchange(e_near, e_far, "tgt")
    r_near, r_far = call(
        end_kernel, [masked], [((H1, cols), bf16)] * 2, [], moved=EST["end"]
    )
    r_near, r_far = exchange(r_near, r_far, "src")
    m_near, m_far, left, src_ends, cost_tgt = call(
        left_kernel,
        [masked, r_near, cost_src, cost_tgt],
        [((rows - 2 * H1, H2), bf16)] * 2
        + [((rows, cols), f32), ((rows, 2 * H1), bf16), (cost_tgt.shape, bf16)],
        [dma((3,))],
        far=(3,),
        moved=EST["left"],
    )
    m_near, m_far = exchange(m_near, m_far, "tgt")
    x_near, x_far = call(
        corner_kernel,
        [e_near, e_far, src_ends],
        [((H1, 2 * H2), bf16)] * 2,
        [],
        moved=EST["corner"],
    )
    x_near, x_far = exchange(x_near, x_far, "src")
    hi, lo = call(
        ends_kernel,
        [left, r_far, src_ends],
        [((rows, cols), bf16)] * 2,
        [],
        moved=EST["ends"],
    )
    grad = call(
        own_kernel, [hi, lo, cost_tgt], [((rows, cols), f32)], [], moved=EST["own"]
    )
    sides = call(
        sides_kernel,
        [e_near, e_far, m_near, m_far, cost_src],
        [((rows, 2 * H2), f32)],
        [],
        moved=EST["sides"],
    )
    kernel, totals = call(
        tail_kernel,
        [x_near, x_far, sides, src_ends, cost_tgt, grad, masked],
        [((rows, cols), f32), ((n_tgt, rows), f32)],
        [VMEM((rows, 2 * H2), bf16)] * 2 + [VMEM((rows, LANES), f32)],
        moved=EST["tail"],
    )
    row_totals = lax.all_to_all(totals, "tgt", 0, 0, tiled=True)
    scaled, totals = call(
        lambda *refs: column_kernel(float(cols * n_tgt), *refs),
        [row_totals, mass_src[None, :], kernel],
        [((rows, cols), f32), ((n_src, cols), f32)],
        [],
        moved=8 * MIB,
    )
    col_totals = lax.all_to_all(totals, "src", 0, 0, tiled=True)
    return call(
        lambda *refs: last_kernel(float(rows * n_src), *refs),
        [col_totals, mass_tgt[None, :], scaled],
        [jax.ShapeDtypeStruct((rows, cols), f32)],
        [VMEM((rows, cols), f32), dma((8,))],
        moved=8 * MIB,
    )


def solution(mesh):
    return jax.shard_map(
        per_device,
        mesh=mesh,
        in_specs=(
            P("src", "tgt"),
            P("src", None),
            P("tgt", None),
            P("src", "tgt"),
            P("src"),
            P("tgt"),
        ),
        out_specs=P("src", "tgt"),
        check_vma=False,
    )
```

```python
import jax
import jax.numpy as jnp
from jax import lax
from jax.experimental import pallas as pl
from jax.experimental.pallas import tpu as pltpu
from jax.sharding import PartitionSpec as P

TILE = 256
H1 = 256
H2 = 256
LANES = 128

step_size = 1.0

f32 = jnp.float32
f8 = jnp.float8_e4m3fn
SCALE = 512.0
bf16 = jnp.bfloat16
VMEM = pltpu.VMEM
MIB = 1 << 20
EST = dict(side=6 * MIB, end=2 * MIB, left=MIB, corner=MIB, ends=MIB, own=MIB, sides=MIB, tail=MIB)


def odd(axis):
    return lax.rem(lax.axis_index(axis), 2) == 1


def at_end(axis):
    index = lax.axis_index(axis)
    return (index == 0) | (index == lax.axis_size(axis) - 1)


def dot(a, b):
    return jnp.dot(a, b, preferred_element_type=f32)


def dot_t(a, b):
    return lax.dot_general(a, b, (((1,), (1,)), ((), ())), preferred_element_type=f32)


def halves(x):
    hi = x.astype(bf16)
    return hi, ((x - hi.astype(f32)) * SCALE).astype(f8)


def two_dots(hi, lo, costs, small):
    return dot_t(hi, costs) + dot_t(lo, small) * (1 / SCALE**2)


def as_row(x):
    return jnp.sum(x.T, axis=0, keepdims=True)


def tiles_of(size):
    return [slice(n * TILE, (n + 1) * TILE) for n in range(size // TILE)]


def side_kernel(pattern, coupling, masked, e_near, e_far, raw, gates, sems, sem):
    rows, cols = masked.shape
    down, along = tiles_of(rows), tiles_of(cols)
    gate = pltpu.make_async_copy(pattern, gates, sem)
    copies = [
        pltpu.make_async_copy(coupling.at[part], raw.at[part], sems.at[r])
        for r, part in enumerate(down)
    ]
    for copy in copies:
        copy.start()
    gate.start()
    odd_t = odd("tgt")
    gate.wait()
    for r, part in enumerate(down):
        copies[r].wait()
        for c, across in enumerate(along):
            tile = raw[part, across]
            masked[part, across] = jnp.where(gates[r, c] != 0, tile, jnp.zeros_like(tile))
        if r in (0, len(down) - 1):
            to = slice(0, H1) if r == 0 else slice(H1, 2 * H1)
            first, last = masked[part, along[0]], masked[part, along[-1]]
            e_near[to, :] = jnp.where(odd_t, first, last)
            e_far[to, :] = jnp.where(odd_t, last, first)


def end_kernel(masked, r_near, r_far):
    rows, cols = masked.shape
    first, last = masked[:H1, :], masked[rows - H1:, :]
    odd_s = odd("src")
    r_near[...] = jnp.where(odd_s, first, last)
    r_far[...] = jnp.where(odd_s, last, first)


def by_nearness(band, own, width, parity, out):
    first, last = band[:, :width], band[:, own + width:]
    out[:, :width] = jnp.where(parity, first, last)
    out[:, width:] = jnp.where(parity, last, first)


def band_copies(band, own, width, parity, out, sems):
    last = own + width
    near = pl.multiple_of((1 - parity) * last, TILE)
    far = pl.multiple_of(parity * last, TILE)
    spans = [(width, own, 0), (near, width, own), (far, width, own + width)]
    return [
        pltpu.make_async_copy(
            band.at[:, pl.ds(start, size)], out.at[:, pl.ds(to, size)], sems.at[n]
        )
        for n, (start, size, to) in enumerate(spans)
    ]


def left_kernel(masked, r_near, cost_src, tgt_hbm,
                m_near, m_far, left, src_ends, cost_tgt, sems):
    rows, cols = masked.shape
    odd_t = odd("tgt")
    copies = band_copies(tgt_hbm, cols, H2, odd_t.astype(jnp.int32), cost_tgt, sems)
    for copy in copies:
        copy.start()
    first, last = masked[H1:rows - H1, :H2], masked[H1:rows - H1, cols - H2:]
    m_near[...] = jnp.where(odd_t, first, last)
    m_far[...] = jnp.where(odd_t, last, first)
    by_nearness(cost_src, rows, H1, odd("src"), src_ends)

    @pl.when(at_end("src"))
    def _():
        src_ends[:, H1:] = jnp.zeros((rows, H1), bf16)

    for across in tiles_of(cols):
        bands = jnp.concatenate([cost_src[:, H1:H1 + rows], src_ends[:, :H1]], axis=1)
        column = jnp.concatenate([masked[:, across], r_near[:, across]], axis=0)
        left[:, across] = dot(bands, column)
    for copy in copies:
        copy.wait()

    @pl.when(at_end("tgt"))
    def _():
        cost_tgt[:, cols + H2:] = jnp.zeros((cols, H2), bf16)


def corner_kernel(e_near, e_far, _, x_near, x_far):
    odd_s = odd("src")
    for n, side in enumerate((e_near, e_far)):
        across = slice(n * H2, (n + 1) * H2)
        first, last = side[:H1, :], side[H1:, :]
        x_near[:, across] = jnp.where(odd_s, first, last)
        x_far[:, across] = jnp.where(odd_s, last, first)


def ends_kernel(left, r_far, src_ends, cost_tgt, hi, lo, small_tgt):
    rows, cols = left.shape
    small_tgt[...] = (cost_tgt[...].astype(f32) * SCALE).astype(f8)
    for across in tiles_of(cols):
        value = left[:, across] + dot(src_ends[:, H1:], r_far[:, across])
        hi[:, across], lo[:, across] = halves(value)


def own_kernel(hi, lo, cost_tgt, small_tgt, grad):
    rows, cols = grad.shape
    for across in tiles_of(cols):
        grad[:, across] = two_dots(
            hi[...], lo[...], cost_tgt[across, :cols], small_tgt[across, :cols]
        )


def sides_kernel(e_near, e_far, m_near, m_far, cost_src, sides):
    rows = cost_src.shape[0]
    for n, (e, m) in enumerate(((e_near, m_near), (e_far, m_far))):
        column = jnp.concatenate([e[:H1, :], m[...], e[H1:, :]], axis=0)
        sides[:, n * H2:(n + 1) * H2] = dot(cost_src[:, H1:H1 + rows], column)


def tail_kernel(x_near, x_far, sides, src_ends, cost_tgt, small_tgt, grad, masked,
                kernel, totals, hi, lo, part):
    rows, cols = masked.shape
    for across in tiles_of(2 * H2):
        corners = jnp.concatenate([x_near[:, across], x_far[:, across]], axis=0)
        hi[:, across], lo[:, across] = halves(sides[:, across] + dot(src_ends[...], corners))
    for n, across in enumerate(tiles_of(cols)):
        slope = grad[:, across] + two_dots(
            hi[...], lo[...], cost_tgt[across, cols:], small_tgt[across, cols:]
        )
        value = masked[:, across].astype(f32) * jnp.exp(step_size * slope)
        kernel[:, across] = value
        sums = value[:, :LANES] + value[:, LANES:]
        part[...] = sums if n == 0 else part[...] + sums
    totals[...] = jnp.broadcast_to(as_row(part[...])[None], totals.shape)


def column_kernel(total, row_totals, mass, kernel, scaled, totals):
    rows, cols = kernel.shape
    factor = mass[...] * total / jnp.sum(row_totals[...], axis=0)
    factor = jnp.broadcast_to(factor, (LANES, rows)).T
    for n in range(cols // LANES):
        across = slice(n * LANES, (n + 1) * LANES)
        value = kernel[:, across] * factor
        scaled[:, across] = value
        sums = jnp.sum(value, axis=0, keepdims=True)
        totals[:, :, across] = jnp.broadcast_to(sums[None], (totals.shape[0], 1, LANES))


def last_kernel(total, col_totals, mass, scaled, out, block, sems):
    rows, cols = scaled.shape
    factor = mass[...] * total / jnp.sum(col_totals[...], axis=0)
    n_blocks = sems.shape[0]
    size = rows // n_blocks

    def copy(n):
        part = pl.ds(n * size, size)
        return pltpu.make_async_copy(block.at[part], out.at[part], sems.at[n])

    for n in range(n_blocks):
        part = slice(n * size, (n + 1) * size)
        block[part, :] = scaled[part, :] * factor
        copy(n).start()
    for n in range(n_blocks):
        copy(n).wait()


def call(body, inputs, outputs, scratch, far=(), limit=12, flops=0, moved=0, exps=0):
    args, in_specs = [], []
    for n, x in enumerate(inputs):
        args.append(pltpu.with_memory_space_constraint(x, pltpu.HBM if n in far else VMEM))
        in_specs.append(pl.BlockSpec(memory_space=pl.ANY if n in far else VMEM))
    is_far = [isinstance(s, jax.ShapeDtypeStruct) for s in outputs]
    shapes = [s if f else VMEM(*s) for s, f in zip(outputs, is_far)]
    out_specs = [pl.BlockSpec(memory_space=pl.ANY if f else VMEM) for f in is_far]
    single = len(outputs) == 1
    return pl.pallas_call(
        body,
        out_shape=shapes[0] if single else shapes,
        in_specs=in_specs,
        out_specs=out_specs[0] if single else out_specs,
        scratch_shapes=scratch,
        cost_estimate=pl.CostEstimate(flops=flops, bytes_accessed=moved, transcendentals=exps),
        compiler_params=pltpu.CompilerParams(vmem_limit_bytes=limit * MIB),
    )(*args)


def pair_plans(size):
    near = [(i, i ^ 1) for i in range(size)]
    far = [(i, (i + 1 if i % 2 else i - 1) % size) for i in range(size)]
    return near, far


def exchange(first, second, axis):
    near, far = pair_plans(lax.axis_size(axis))
    return lax.ppermute(first, axis, near), lax.ppermute(second, axis, far)


def per_device(coupling, cost_src, cost_tgt, pattern, mass_src, mass_tgt):
    rows, cols = coupling.shape
    n_src, n_tgt = lax.axis_size("src"), lax.axis_size("tgt")
    tiles = pattern.shape[0]
    dma = pltpu.SemaphoreType.DMA

    masked, e_near, e_far = call(
        side_kernel,
        [pattern, coupling],
        [((rows, cols), bf16)] + [((2 * H1, H2), bf16)] * 2,
        [
            VMEM((rows, cols), bf16),
            pltpu.SMEM(pattern.shape, pattern.dtype),
            dma((tiles,)),
            dma,
        ],
        far=(0, 1),
        moved=EST["side"],
    )
    e_near, e_far = exchange(e_near, e_far, "tgt")
    r_near, r_far = call(
        end_kernel, [masked], [((H1, cols), bf16)] * 2, [], moved=EST["end"]
    )
    r_near, r_far = exchange(r_near, r_far, "src")
    m_near, m_far, left, src_ends, cost_tgt = call(
        left_kernel,
        [masked, r_near, cost_src, cost_tgt],
        [((rows - 2 * H1, H2), bf16)] * 2
        + [((rows, cols), f32), ((rows, 2 * H1), bf16), (cost_tgt.shape, bf16)],
        [dma((3,))],
        far=(3,),
        moved=EST["left"],
    )
    m_near, m_far = exchange(m_near, m_far, "tgt")
    hi, lo, small_tgt = call(
        ends_kernel,
        [left, r_far, src_ends, cost_tgt],
        [((rows, cols), bf16), ((rows, cols), f8), (cost_tgt.shape, f8)],
        [],
        moved=EST["ends"],
    )
    x_near, x_far = call(
        corner_kernel,
        [e_near, e_far, lo],
        [((H1, 2 * H2), bf16)] * 2,
        [],
        moved=EST["corner"],
    )
    x_near, x_far = exchange(x_near, x_far, "src")
    grad = call(
        own_kernel, [hi, lo, cost_tgt, small_tgt], [((rows, cols), f32)], [], moved=EST["own"]
    )
    sides = call(
        sides_kernel,
        [e_near, e_far, m_near, m_far, cost_src],
        [((rows, 2 * H2), f32)],
        [],
        moved=EST["sides"],
    )
    kernel, totals = call(
        tail_kernel,
        [x_near, x_far, sides, src_ends, cost_tgt, small_tgt, grad, masked],
        [((rows, cols), f32), ((n_tgt, 1, rows), f32)],
        [VMEM((rows, 2 * H2), bf16), VMEM((rows, 2 * H2), f8), VMEM((rows, LANES), f32)],
        moved=EST["tail"],
    )
    row_totals = lax.all_to_all(totals, "tgt", 0, 0, tiled=True)
    scaled, totals = call(
        lambda *refs: column_kernel(float(cols * n_tgt), *refs),
        [row_totals, mass_src[None, :], kernel],
        [((rows, cols), f32), ((n_src, 1, cols), f32)],
        [],
        moved=8 * MIB,
    )
    col_totals = lax.all_to_all(totals, "src", 0, 0, tiled=True)
    return call(
        lambda *refs: last_kernel(float(rows * n_src), *refs),
        [col_totals, mass_tgt[None, :], scaled],
        [jax.ShapeDtypeStruct((rows, cols), f32)],
        [VMEM((rows, cols), f32), dma((8,))],
        moved=8 * MIB,
    )


def solution(mesh):
    return jax.shard_map(
        per_device,
        mesh=mesh,
        in_specs=(
            P("src", "tgt"),
            P("src", None),
            P("tgt", None),
            P("src", "tgt"),
            P("src"),
            P("tgt"),
        ),
        out_specs=P("src", "tgt"),
        check_vma=False,
    )
```

```python
import jax
import jax.numpy as jnp
from jax import lax
from jax.experimental import pallas as pl
from jax.experimental.pallas import tpu as pltpu
from jax.sharding import PartitionSpec as P

TILE = 256
H1 = 256
H2 = 256
LANES = 128

step_size = 1.0

f32 = jnp.float32
f8 = jnp.float8_e4m3fn
SCALE = 512.0
bf16 = jnp.bfloat16
VMEM = pltpu.VMEM
MIB = 1 << 20
EST = dict(side=6 * MIB, end=2 * MIB, left=MIB, corner=MIB, ends=MIB, own=MIB, sides=MIB, tail=MIB)


def odd(axis):
    return lax.rem(lax.axis_index(axis), 2) == 1


def at_end(axis):
    index = lax.axis_index(axis)
    return (index == 0) | (index == lax.axis_size(axis) - 1)


def dot(a, b):
    return jnp.dot(a, b, preferred_element_type=f32)


def dot_t(a, b):
    return lax.dot_general(a, b, (((1,), (1,)), ((), ())), preferred_element_type=f32)


def halves(x):
    hi = x.astype(bf16)
    return hi, ((x - hi.astype(f32)) * SCALE).astype(f8)


def two_dots(hi, lo, costs, small):
    return dot_t(hi, costs) + dot_t(lo, small) * (1 / SCALE**2)


def as_row(x):
    return jnp.sum(x.T, axis=0, keepdims=True)


def tiles_of(size):
    return [slice(n * TILE, (n + 1) * TILE) for n in range(size // TILE)]


def side_kernel(pattern, coupling, masked, e_near, e_far, raw, gates, sems, sem):
    rows, cols = masked.shape
    down, along = tiles_of(rows), tiles_of(cols)
    gate = pltpu.make_async_copy(pattern, gates, sem)
    copies = [
        pltpu.make_async_copy(coupling.at[part], raw.at[part], sems.at[r])
        for r, part in enumerate(down)
    ]
    for copy in copies:
        copy.start()
    gate.start()
    odd_t = odd("tgt")
    gate.wait()
    for r, part in enumerate(down):
        copies[r].wait()
        for c, across in enumerate(along):
            tile = raw[part, across]
            masked[part, across] = jnp.where(gates[r, c] != 0, tile, jnp.zeros_like(tile))
        if r in (0, len(down) - 1):
            to = slice(0, H1) if r == 0 else slice(H1, 2 * H1)
            first, last = masked[part, along[0]], masked[part, along[-1]]
            e_near[to, :] = jnp.where(odd_t, first, last)
            e_far[to, :] = jnp.where(odd_t, last, first)


def end_kernel(masked, r_near, r_far):
    rows, cols = masked.shape
    first, last = masked[:H1, :], masked[rows - H1:, :]
    odd_s = odd("src")
    r_near[...] = jnp.where(odd_s, first, last)
    r_far[...] = jnp.where(odd_s, last, first)


def by_nearness(band, own, width, parity, out):
    first, last = band[:, :width], band[:, own + width:]
    out[:, :width] = jnp.where(parity, first, last)
    out[:, width:] = jnp.where(parity, last, first)


def band_copies(band, own, width, parity, out, sems):
    last = own + width
    near = pl.multiple_of((1 - parity) * last, TILE)
    far = pl.multiple_of(parity * last, TILE)
    spans = [(width, own, 0), (near, width, own), (far, width, own + width)]
    return [
        pltpu.make_async_copy(
            band.at[:, pl.ds(start, size)], out.at[:, pl.ds(to, size)], sems.at[n]
        )
        for n, (start, size, to) in enumerate(spans)
    ]


def left_kernel(masked, r_near, cost_src, tgt_hbm,
                m_near, m_far, left, src_ends, cost_tgt, sems):
    rows, cols = masked.shape
    odd_t = odd("tgt")
    copies = band_copies(tgt_hbm, cols, H2, odd_t.astype(jnp.int32), cost_tgt, sems)
    for copy in copies:
        copy.start()
    first, last = masked[H1:rows - H1, :H2], masked[H1:rows - H1, cols - H2:]
    m_near[...] = jnp.where(odd_t, first, last)
    m_far[...] = jnp.where(odd_t, last, first)
    by_nearness(cost_src, rows, H1, odd("src"), src_ends)

    @pl.when(at_end("src"))
    def _():
        src_ends[:, H1:] = jnp.zeros((rows, H1), bf16)

    for across in tiles_of(cols):
        bands = jnp.concatenate([cost_src[:, H1:H1 + rows], src_ends[:, :H1]], axis=1)
        column = jnp.concatenate([masked[:, across], r_near[:, across]], axis=0)
        left[:, across] = dot(bands, column)
    for copy in copies:
        copy.wait()

    @pl.when(at_end("tgt"))
    def _():
        cost_tgt[:, cols + H2:] = jnp.zeros((cols, H2), bf16)


def corner_kernel(e_near, e_far, _, x_near, x_far):
    odd_s = odd("src")
    for n, side in enumerate((e_near, e_far)):
        across = slice(n * H2, (n + 1) * H2)
        first, last = side[:H1, :], side[H1:, :]
        x_near[:, across] = jnp.where(odd_s, first, last)
        x_far[:, across] = jnp.where(odd_s, last, first)


def small_kernel(cost_tgt, small_tgt):
    small_tgt[...] = (cost_tgt[...].astype(f32) * SCALE).astype(f8)


def ends_kernel(left, r_far, src_ends, _, hi, lo):
    rows, cols = left.shape
    for across in tiles_of(cols):
        value = left[:, across] + dot(src_ends[:, H1:], r_far[:, across])
        hi[:, across], lo[:, across] = halves(value)


def own_kernel(hi, lo, cost_tgt, small_tgt, grad):
    rows, cols = grad.shape
    for across in tiles_of(cols):
        grad[:, across] = two_dots(
            hi[...], lo[...], cost_tgt[across, :cols], small_tgt[across, :cols]
        )


def sides_kernel(e_near, e_far, m_near, m_far, cost_src, sides):
    rows = cost_src.shape[0]
    for n, (e, m) in enumerate(((e_near, m_near), (e_far, m_far))):
        column = jnp.concatenate([e[:H1, :], m[...], e[H1:, :]], axis=0)
        sides[:, n * H2:(n + 1) * H2] = dot(cost_src[:, H1:H1 + rows], column)


def tail_kernel(x_near, x_far, sides, src_ends, cost_tgt, small_tgt, grad, masked,
                kernel, totals, hi, lo, part):
    rows, cols = masked.shape
    for across in tiles_of(2 * H2):
        corners = jnp.concatenate([x_near[:, across], x_far[:, across]], axis=0)
        hi[:, across], lo[:, across] = halves(sides[:, across] + dot(src_ends[...], corners))
    for n, across in enumerate(tiles_of(cols)):
        slope = grad[:, across] + two_dots(
            hi[...], lo[...], cost_tgt[across, cols:], small_tgt[across, cols:]
        )
        value = masked[:, across].astype(f32) * jnp.exp(step_size * slope)
        kernel[:, across] = value
        sums = value[:, :LANES] + value[:, LANES:]
        part[...] = sums if n == 0 else part[...] + sums
    totals[...] = jnp.broadcast_to(as_row(part[...])[None], totals.shape)


def column_kernel(total, row_totals, mass, kernel, scaled, totals):
    rows, cols = kernel.shape
    factor = mass[...] * total / jnp.sum(row_totals[...], axis=0)
    factor = jnp.broadcast_to(factor, (LANES, rows)).T
    for n in range(cols // LANES):
        across = slice(n * LANES, (n + 1) * LANES)
        value = kernel[:, across] * factor
        scaled[:, across] = value
        sums = jnp.sum(value, axis=0, keepdims=True)
        totals[:, :, across] = jnp.broadcast_to(sums[None], (totals.shape[0], 1, LANES))


def last_kernel(total, col_totals, mass, scaled, out, block, sems):
    rows, cols = scaled.shape
    factor = mass[...] * total / jnp.sum(col_totals[...], axis=0)
    n_blocks = sems.shape[0]
    size = rows // n_blocks

    def copy(n):
        part = pl.ds(n * size, size)
        return pltpu.make_async_copy(block.at[part], out.at[part], sems.at[n])

    for n in range(n_blocks):
        part = slice(n * size, (n + 1) * size)
        block[part, :] = scaled[part, :] * factor
        copy(n).start()
    for n in range(n_blocks):
        copy(n).wait()


def call(body, inputs, outputs, scratch, far=(), limit=12, flops=0, moved=0, exps=0):
    args, in_specs = [], []
    for n, x in enumerate(inputs):
        args.append(pltpu.with_memory_space_constraint(x, pltpu.HBM if n in far else VMEM))
        in_specs.append(pl.BlockSpec(memory_space=pl.ANY if n in far else VMEM))
    is_far = [isinstance(s, jax.ShapeDtypeStruct) for s in outputs]
    shapes = [s if f else VMEM(*s) for s, f in zip(outputs, is_far)]
    out_specs = [pl.BlockSpec(memory_space=pl.ANY if f else VMEM) for f in is_far]
    single = len(outputs) == 1
    return pl.pallas_call(
        body,
        out_shape=shapes[0] if single else shapes,
        in_specs=in_specs,
        out_specs=out_specs[0] if single else out_specs,
        scratch_shapes=scratch,
        cost_estimate=pl.CostEstimate(flops=flops, bytes_accessed=moved, transcendentals=exps),
        compiler_params=pltpu.CompilerParams(vmem_limit_bytes=limit * MIB),
    )(*args)


def far_of(index, size):
    return (index + 1 if index % 2 else index - 1) % size


def exchange(first, second, axis):
    n_src, n_tgt = lax.axis_size("src"), lax.axis_size("tgt")
    size = lax.axis_size(axis)
    near = [(i, i ^ 1) for i in range(size)]
    far = []
    for s in range(n_src):
        for t in range(n_tgt):
            to = (s, far_of(t, n_tgt)) if axis == "tgt" else (far_of(s, n_src), t)
            if axis == "tgt" and t in (0, n_tgt - 1):
                to = (s ^ 1, t)
            far.append((s * n_tgt + t, to[0] * n_tgt + to[1]))
    return lax.ppermute(first, axis, near), lax.ppermute(second, ("src", "tgt"), far)


def per_device(coupling, cost_src, cost_tgt, pattern, mass_src, mass_tgt):
    rows, cols = coupling.shape
    n_src, n_tgt = lax.axis_size("src"), lax.axis_size("tgt")
    tiles = pattern.shape[0]
    dma = pltpu.SemaphoreType.DMA

    masked, e_near, e_far = call(
        side_kernel,
        [pattern, coupling],
        [((rows, cols), bf16)] + [((2 * H1, H2), bf16)] * 2,
        [
            VMEM((rows, cols), bf16),
            pltpu.SMEM(pattern.shape, pattern.dtype),
            dma((tiles,)),
            dma,
        ],
        far=(0, 1),
        moved=EST["side"],
    )
    e_near, e_far = exchange(e_near, e_far, "tgt")
    r_near, r_far = call(
        end_kernel, [masked], [((H1, cols), bf16)] * 2, [], moved=EST["end"]
    )
    r_near, r_far = exchange(r_near, r_far, "src")
    m_near, m_far, left, src_ends, cost_tgt = call(
        left_kernel,
        [masked, r_near, cost_src, cost_tgt],
        [((rows - 2 * H1, H2), bf16)] * 2
        + [((rows, cols), f32), ((rows, 2 * H1), bf16), (cost_tgt.shape, bf16)],
        [dma((3,))],
        far=(3,),
        moved=EST["left"],
    )
    m_near, m_far = exchange(m_near, m_far, "tgt")
    small_tgt = call(small_kernel, [cost_tgt], [(cost_tgt.shape, f8)], [], moved=MIB)
    hi, lo = call(
        ends_kernel,
        [left, r_far, src_ends, small_tgt],
        [((rows, cols), bf16), ((rows, cols), f8)],
        [],
        moved=EST["ends"],
    )
    x_near, x_far = call(
        corner_kernel,
        [e_near, e_far, lo],
        [((H1, 2 * H2), bf16)] * 2,
        [],
        moved=EST["corner"],
    )
    x_near, x_far = exchange(x_near, x_far, "src")
    grad = call(
        own_kernel, [hi, lo, cost_tgt, small_tgt], [((rows, cols), f32)], [], moved=EST["own"]
    )
    sides = call(
        sides_kernel,
        [e_near, e_far, m_near, m_far, cost_src],
        [((rows, 2 * H2), f32)],
        [],
        moved=EST["sides"],
    )
    kernel, totals = call(
        tail_kernel,
        [x_near, x_far, sides, src_ends, cost_tgt, small_tgt, grad, masked],
        [((rows, cols), f32), ((n_tgt, 1, rows), f32)],
        [VMEM((rows, 2 * H2), bf16), VMEM((rows, 2 * H2), f8), VMEM((rows, LANES), f32)],
        moved=EST["tail"],
    )
    row_totals = lax.all_to_all(totals, "tgt", 0, 0, tiled=True)
    scaled, totals = call(
        lambda *refs: column_kernel(float(cols * n_tgt), *refs),
        [row_totals, mass_src[None, :], kernel],
        [((rows, cols), f32), ((n_src, 1, cols), f32)],
        [],
        moved=8 * MIB,
    )
    col_totals = lax.all_to_all(totals, "src", 0, 0, tiled=True)
    return call(
        lambda *refs: last_kernel(float(rows * n_src), *refs),
        [col_totals, mass_tgt[None, :], scaled],
        [jax.ShapeDtypeStruct((rows, cols), f32)],
        [VMEM((rows, cols), f32), dma((8,))],
        moved=8 * MIB,
    )


def solution(mesh):
    return jax.shard_map(
        per_device,
        mesh=mesh,
        in_specs=(
            P("src", "tgt"),
            P("src", None),
            P("tgt", None),
            P("src", "tgt"),
            P("src"),
            P("tgt"),
        ),
        out_specs=P("src", "tgt"),
        check_vma=False,
    )
```

```python
import jax
import jax.numpy as jnp
from jax import lax
from jax.experimental import pallas as pl
from jax.experimental.pallas import tpu as pltpu
from jax.sharding import PartitionSpec as P

TILE = 256
H1 = 256
H2 = 256
LANES = 128

step_size = 1.0

f32 = jnp.float32
f8 = jnp.float8_e4m3fn
SCALE = 512.0
bf16 = jnp.bfloat16
VMEM = pltpu.VMEM
MIB = 1 << 20
EST = dict(side=6 * MIB, end=2 * MIB, left=MIB, corner=MIB, ends=MIB, own=MIB, sides=MIB, tail=MIB)


def odd(axis):
    return lax.rem(lax.axis_index(axis), 2) == 1


def at_end(axis):
    index = lax.axis_index(axis)
    return (index == 0) | (index == lax.axis_size(axis) - 1)


def dot(a, b):
    return jnp.dot(a, b, preferred_element_type=f32)


def dot_t(a, b):
    return lax.dot_general(a, b, (((1,), (1,)), ((), ())), preferred_element_type=f32)


def halves(x):
    hi = x.astype(bf16)
    return hi, ((x - hi.astype(f32)) * SCALE).astype(f8)


def two_dots(hi, lo, costs, small):
    return dot_t(hi, costs) + dot_t(lo, small) * (1 / SCALE**2)


def as_row(x):
    return jnp.sum(x.T, axis=0, keepdims=True)


def tiles_of(size):
    return [slice(n * TILE, (n + 1) * TILE) for n in range(size // TILE)]


def side_kernel(pattern, coupling, masked, e_near, e_far, raw, gates, sems, sem):
    rows, cols = masked.shape
    down, along = tiles_of(rows), tiles_of(cols)
    gate = pltpu.make_async_copy(pattern, gates, sem)
    copies = [
        pltpu.make_async_copy(coupling.at[part], raw.at[part], sems.at[r])
        for r, part in enumerate(down)
    ]
    for copy in copies:
        copy.start()
    gate.start()
    odd_t = odd("tgt")
    gate.wait()
    for r, part in enumerate(down):
        copies[r].wait()
        for c, across in enumerate(along):
            tile = raw[part, across]
            masked[part, across] = jnp.where(gates[r, c] != 0, tile, jnp.zeros_like(tile))
        if r in (0, len(down) - 1):
            to = slice(0, H1) if r == 0 else slice(H1, 2 * H1)
            first, last = masked[part, along[0]], masked[part, along[-1]]
            e_near[to, :] = jnp.where(odd_t, first, last)
            e_far[to, :] = jnp.where(odd_t, last, first)


def end_kernel(masked, r_near, r_far):
    rows, cols = masked.shape
    first, last = masked[:H1, :], masked[rows - H1:, :]
    odd_s = odd("src")
    r_near[...] = jnp.where(odd_s, first, last)
    r_far[...] = jnp.where(odd_s, last, first)


def by_nearness(band, own, width, parity, out):
    first, last = band[:, :width], band[:, own + width:]
    out[:, :width] = jnp.where(parity, first, last)
    out[:, width:] = jnp.where(parity, last, first)


def band_copies(band, own, width, parity, out, sems):
    last = own + width
    near = pl.multiple_of((1 - parity) * last, TILE)
    far = pl.multiple_of(parity * last, TILE)
    spans = [(width, own, 0), (near, width, own), (far, width, own + width)]
    return [
        pltpu.make_async_copy(
            band.at[:, pl.ds(start, size)], out.at[:, pl.ds(to, size)], sems.at[n]
        )
        for n, (start, size, to) in enumerate(spans)
    ]


def left_kernel(masked, r_near, cost_src, tgt_hbm,
                m_near, m_far, left, src_ends, cost_tgt, sems):
    rows, cols = masked.shape
    odd_t = odd("tgt")
    copies = band_copies(tgt_hbm, cols, H2, odd_t.astype(jnp.int32), cost_tgt, sems)
    for copy in copies:
        copy.start()
    first, last = masked[H1:rows - H1, :H2], masked[H1:rows - H1, cols - H2:]
    m_near[...] = jnp.where(odd_t, first, last)
    m_far[...] = jnp.where(odd_t, last, first)
    by_nearness(cost_src, rows, H1, odd("src"), src_ends)

    @pl.when(at_end("src"))
    def _():
        src_ends[:, H1:] = jnp.zeros((rows, H1), bf16)

    for across in tiles_of(cols):
        bands = jnp.concatenate([cost_src[:, H1:H1 + rows], src_ends[:, :H1]], axis=1)
        column = jnp.concatenate([masked[:, across], r_near[:, across]], axis=0)
        left[:, across] = dot(bands, column)
    for copy in copies:
        copy.wait()

    @pl.when(at_end("tgt"))
    def _():
        cost_tgt[:, cols + H2:] = jnp.zeros((cols, H2), bf16)


def corner_kernel(e_near, e_far, _, x_near, x_far):
    odd_s = odd("src")
    for n, side in enumerate((e_near, e_far)):
        across = slice(n * H2, (n + 1) * H2)
        first, last = side[:H1, :], side[H1:, :]
        x_near[:, across] = jnp.where(odd_s, first, last)
        x_far[:, across] = jnp.where(odd_s, last, first)


def small_kernel(cost_tgt, small_tgt):
    small_tgt[...] = (cost_tgt[...].astype(f32) * SCALE).astype(f8)


def ends_kernel(left, r_far, src_ends, _, hi, lo):
    rows, cols = left.shape
    for across in tiles_of(cols):
        value = left[:, across] + dot(src_ends[:, H1:], r_far[:, across])
        hi[:, across], lo[:, across] = halves(value)


def own_kernel(hi, lo, cost_tgt, small_tgt, grad):
    rows, cols = grad.shape
    for across in tiles_of(cols):
        grad[:, across] = two_dots(
            hi[...], lo[...], cost_tgt[across, :cols], small_tgt[across, :cols]
        )


def sides_kernel(e_near, e_far, m_near, m_far, cost_src, sides):
    rows = cost_src.shape[0]
    for n, (e, m) in enumerate(((e_near, m_near), (e_far, m_far))):
        column = jnp.concatenate([e[:H1, :], m[...], e[H1:, :]], axis=0)
        sides[:, n * H2:(n + 1) * H2] = dot(cost_src[:, H1:H1 + rows], column)


def tail_kernel(x_near, x_far, sides, src_ends, cost_tgt, small_tgt, grad, masked,
                kernel, totals, hi, lo, part):
    rows, cols = masked.shape
    for across in tiles_of(2 * H2):
        corners = jnp.concatenate([x_near[:, across], x_far[:, across]], axis=0)
        hi[:, across], lo[:, across] = halves(sides[:, across] + dot(src_ends[...], corners))
    for n, across in enumerate(tiles_of(cols)):
        slope = grad[:, across] + two_dots(
            hi[...], lo[...], cost_tgt[across, cols:], small_tgt[across, cols:]
        )
        value = masked[:, across].astype(f32) * jnp.exp(step_size * slope)
        kernel[:, across] = value
        sums = value[:, :LANES] + value[:, LANES:]
        part[...] = sums if n == 0 else part[...] + sums
    totals[...] = jnp.broadcast_to(as_row(part[...])[None], totals.shape)


def column_kernel(total, row_totals, mass, kernel, rows_by, totals):
    rows, cols = kernel.shape
    factor = mass[...] * total / jnp.sum(row_totals[...], axis=0)
    factor = jnp.broadcast_to(factor, (LANES, rows)).T
    rows_by[...] = factor
    for n in range(cols // LANES):
        across = slice(n * LANES, (n + 1) * LANES)
        sums = jnp.sum(kernel[:, across] * factor, axis=0, keepdims=True)
        totals[:, :, across] = jnp.broadcast_to(sums[None], (totals.shape[0], 1, LANES))


def last_kernel(total, col_totals, mass, rows_by, kernel, out, block, sems):
    rows, cols = kernel.shape
    factor = mass[...] * total / jnp.sum(col_totals[...], axis=0)
    n_blocks = sems.shape[0]
    size = rows // n_blocks

    def copy(n):
        part = pl.ds(n * size, size)
        return pltpu.make_async_copy(block.at[part], out.at[part], sems.at[n])

    for n in range(n_blocks):
        part = slice(n * size, (n + 1) * size)
        for k in range(cols // LANES):
            across = slice(k * LANES, (k + 1) * LANES)
            block[part, across] = kernel[part, across] * rows_by[part, :] * factor[:, across]
        copy(n).start()
    for n in range(n_blocks):
        copy(n).wait()


def call(body, inputs, outputs, scratch, far=(), limit=12, flops=0, moved=0, exps=0):
    args, in_specs = [], []
    for n, x in enumerate(inputs):
        args.append(pltpu.with_memory_space_constraint(x, pltpu.HBM if n in far else VMEM))
        in_specs.append(pl.BlockSpec(memory_space=pl.ANY if n in far else VMEM))
    is_far = [isinstance(s, jax.ShapeDtypeStruct) for s in outputs]
    shapes = [s if f else VMEM(*s) for s, f in zip(outputs, is_far)]
    out_specs = [pl.BlockSpec(memory_space=pl.ANY if f else VMEM) for f in is_far]
    single = len(outputs) == 1
    return pl.pallas_call(
        body,
        out_shape=shapes[0] if single else shapes,
        in_specs=in_specs,
        out_specs=out_specs[0] if single else out_specs,
        scratch_shapes=scratch,
        cost_estimate=pl.CostEstimate(flops=flops, bytes_accessed=moved, transcendentals=exps),
        compiler_params=pltpu.CompilerParams(vmem_limit_bytes=limit * MIB),
    )(*args)


def far_of(index, size):
    return (index + 1 if index % 2 else index - 1) % size


def exchange(first, second, axis):
    n_src, n_tgt = lax.axis_size("src"), lax.axis_size("tgt")
    size = lax.axis_size(axis)
    near = [(i, i ^ 1) for i in range(size)]
    far = []
    for s in range(n_src):
        for t in range(n_tgt):
            to = (s, far_of(t, n_tgt)) if axis == "tgt" else (far_of(s, n_src), t)
            if axis == "tgt" and t in (0, n_tgt - 1):
                to = (s ^ 1, t)
            far.append((s * n_tgt + t, to[0] * n_tgt + to[1]))
    return lax.ppermute(first, axis, near), lax.ppermute(second, ("src", "tgt"), far)


def per_device(coupling, cost_src, cost_tgt, pattern, mass_src, mass_tgt):
    rows, cols = coupling.shape
    n_src, n_tgt = lax.axis_size("src"), lax.axis_size("tgt")
    tiles = pattern.shape[0]
    dma = pltpu.SemaphoreType.DMA

    masked, e_near, e_far = call(
        side_kernel,
        [pattern, coupling],
        [((rows, cols), bf16)] + [((2 * H1, H2), bf16)] * 2,
        [
            VMEM((rows, cols), bf16),
            pltpu.SMEM(pattern.shape, pattern.dtype),
            dma((tiles,)),
            dma,
        ],
        far=(0, 1),
        moved=EST["side"],
    )
    e_near, e_far = exchange(e_near, e_far, "tgt")
    r_near, r_far = call(
        end_kernel, [masked], [((H1, cols), bf16)] * 2, [], moved=EST["end"]
    )
    r_near, r_far = exchange(r_near, r_far, "src")
    m_near, m_far, left, src_ends, cost_tgt = call(
        left_kernel,
        [masked, r_near, cost_src, cost_tgt],
        [((rows - 2 * H1, H2), bf16)] * 2
        + [((rows, cols), f32), ((rows, 2 * H1), bf16), (cost_tgt.shape, bf16)],
        [dma((3,))],
        far=(3,),
        moved=EST["left"],
    )
    m_near, m_far = exchange(m_near, m_far, "tgt")
    small_tgt = call(small_kernel, [cost_tgt], [(cost_tgt.shape, f8)], [], moved=MIB)
    hi, lo = call(
        ends_kernel,
        [left, r_far, src_ends, small_tgt],
        [((rows, cols), bf16), ((rows, cols), f8)],
        [],
        moved=EST["ends"],
    )
    x_near, x_far = call(
        corner_kernel,
        [e_near, e_far, lo],
        [((H1, 2 * H2), bf16)] * 2,
        [],
        moved=EST["corner"],
    )
    x_near, x_far = exchange(x_near, x_far, "src")
    grad = call(
        own_kernel, [hi, lo, cost_tgt, small_tgt], [((rows, cols), f32)], [], moved=EST["own"]
    )
    sides = call(
        sides_kernel,
        [e_near, e_far, m_near, m_far, cost_src],
        [((rows, 2 * H2), f32)],
        [],
        moved=EST["sides"],
    )
    kernel, totals = call(
        tail_kernel,
        [x_near, x_far, sides, src_ends, cost_tgt, small_tgt, grad, masked],
        [((rows, cols), f32), ((n_tgt, 1, rows), f32)],
        [VMEM((rows, 2 * H2), bf16), VMEM((rows, 2 * H2), f8), VMEM((rows, LANES), f32)],
        moved=EST["tail"],
    )
    row_totals = lax.all_to_all(totals, "tgt", 0, 0, tiled=True)
    rows_by, totals = call(
        lambda *refs: column_kernel(float(cols * n_tgt), *refs),
        [row_totals, mass_src[None, :], kernel],
        [((rows, LANES), f32), ((n_src, 1, cols), f32)],
        [],
        moved=8 * MIB,
    )
    col_totals = lax.all_to_all(totals, "src", 0, 0, tiled=True)
    return call(
        lambda *refs: last_kernel(float(rows * n_src), *refs),
        [col_totals, mass_tgt[None, :], rows_by, kernel],
        [jax.ShapeDtypeStruct((rows, cols), f32)],
        [VMEM((rows, cols), f32), dma((8,))],
        moved=8 * MIB,
    )


def solution(mesh):
    return jax.shard_map(
        per_device,
        mesh=mesh,
        in_specs=(
            P("src", "tgt"),
            P("src", None),
            P("tgt", None),
            P("src", "tgt"),
            P("src"),
            P("tgt"),
        ),
        out_specs=P("src", "tgt"),
        check_vma=False,
    )
```
